256 devices in a mesh: panel: 32 (over x, z_hi, core), freq: 8 (over z_lo, y).
Axes of the slice: x: 4, y: 4, z: 8 (z_hi: 4, z_lo: 2; z = z_hi * 2 + z_lo), core: 2. Of those that a mesh axis runs over, the one named last changes fastest.
Arguments:
- sources: bfloat16 [2, 8192, 1024], P(None, ('panel', 'freq')), may hold values from -6 to 6
- panel_pos: float32 [3, 8192], P(None, 'panel'), may hold values from -30 to 30
- normal_angles: float32 [2, 8192], P(None, 'panel'), may hold values from -3.140625 to 3.140625
- observer_angles: float32 [2, 2048], replicated, may hold values from -3.140625 to 3.140625
- absorption: float32 [64, 16], replicated, may hold values from 0.05 to 1
- ray_count: int32 [131072], P('panel'), may hold values from 1 to 8
- ray_layer: int32 [8, 131072], P(None, 'panel'), may hold values from 0 to 15
- ray_length: float32 [8, 131072], P(None, 'panel'), may hold values from 0.1 to 1
- ray_weight: float32 [131072], P('panel'), may hold values from 0.01 to 0.1
- ray_ground: int32 [131072], P('panel'), may hold values from 0 to 4095
Outputs:
- obs_spectrum: float32 [2048, 128], P('panel', 'freq')
- ground_power: float32 [64, 4096], P(None, 'panel')
The draws below stay inside these ranges and needn't reach their ends.
All inputs are finite; a program needn't handle non-finite values.
Results may differ from the reference program's by a relative error of at most 0.0026.
Values may be sent and summed in bfloat16 or wider, within the bound.
No kernel may reach another device: no remote copies, remote signals or barrier semaphores. Data moves between devices by JAX's collectives and lax.ppermute only.
A program may use at most 64 MiB of HBM per device.

```python
import math
import jax
import jax.numpy as jnp
from jax import lax

SAMPLES = 1024
FREQS = 64
BIN0 = 32
OBS = 2048
PANELS = 8192
RAYS = 64
RAY_ROWS = 131072
SEGS = 8
LAYERS = 16
GROUND = 4096


def plant(array, rng, least, top_value):
    longest = array.shape.index(max(array.shape))
    spots = []
    for shift in (0, 1):
        where = [jax.random.randint(jax.random.fold_in(rng, axis), (), 0, length) for axis, length in enumerate(array.shape)]
        where[longest] = (where[longest] + shift) % array.shape[longest]
        spots.append(tuple(where))
    return array.at[spots[0]].set(least).at[spots[1]].set(top_value)


def level_of(own_key, extent, split, low, high):
    loudness = 1.0
    for position, parts in split:
        draws = jax.random.uniform(jax.random.fold_in(jax.random.fold_in(own_key, 6), position), (parts,), jnp.float32, low / len(split), high / len(split))
        loudness = loudness * jnp.repeat(jnp.exp(draws), extent[position] // parts).reshape((-1,) + (1,) * (len(extent) - 1 - position))
    return loudness


def gaussian(rng, dims, width, reach, split=(), held_as=jnp.bfloat16):
    factor_of = level_of(rng, dims, split, -0.22, 0.18) if split else 1.0
    values = jax.random.normal(rng, dims, jnp.float32) * width * factor_of
    return jnp.minimum(jnp.maximum(values, -reach), reach).astype(held_as)


def setup_inputs(seed: int = 0) -> dict:
    splits = jax.random.split(jax.random.key(seed), 11)
    sources = gaussian(splits[0], (2, PANELS, SAMPLES), 1.0, 6.0, ((1, 256),))
    panel_pos = jnp.clip(jax.random.uniform(splits[1], (3, PANELS), jnp.float32, -30.0, 30.0) * level_of(splits[1], (3, PANELS), ((1, 32),), -0.4, 0.0), -30.0, 30.0)
    normal_angles = jnp.clip(jax.random.uniform(splits[2], (2, PANELS), jnp.float32, -3.140625, 3.140625), -3.140625, 3.140625)
    observer_angles = jnp.clip(jax.random.uniform(splits[3], (2, OBS), jnp.float32, -3.140625, 3.140625), -3.140625, 3.140625)
    absorption = jnp.clip(jnp.exp(jax.random.uniform(splits[4], (FREQS, LAYERS), jnp.float32, math.log(0.05), math.log(1.0))), 0.05, 1.0)
    ray_count = plant(jax.random.randint(splits[5], (RAY_ROWS,), 1, SEGS + 1), jax.random.fold_in(splits[5], 1), 1, SEGS).astype(jnp.int32)
    ray_layer = plant(jax.random.randint(splits[6], (SEGS, RAY_ROWS), 0, LAYERS), jax.random.fold_in(splits[6], 1), 0, LAYERS - 1).astype(jnp.int32)
    ray_length = jnp.clip(jnp.exp(math.log(1.0) - 2.3025851 * jax.random.uniform(splits[7], (SEGS, RAY_ROWS), jnp.float32) ** level_of(splits[7], (SEGS, RAY_ROWS), ((1, 32),), -0.2, 0.2)), 0.1, 1.0)
    ray_weight = jnp.clip(jnp.exp(math.log(0.1) - 2.3025851 * jax.random.uniform(splits[8], (RAY_ROWS,), jnp.float32) ** level_of(splits[8], (RAY_ROWS,), ((0, 32),), -0.2, 0.2)), 0.01, 0.1)
    ray_ground = plant(jax.random.randint(splits[9], (RAY_ROWS,), 0, GROUND), jax.random.fold_in(splits[9], 1), 0, GROUND - 1).astype(jnp.int32)
    return dict(sources=sources, panel_pos=panel_pos, normal_angles=normal_angles, observer_angles=observer_angles, absorption=absorption, ray_count=ray_count, ray_layer=ray_layer, ray_length=ray_length, ray_weight=ray_weight, ray_ground=ray_ground)


RADIUS = 150.0
GAIN = 3.0

def dft_table(samples, first_bin, nfreqs):
    sample_index = jnp.arange(samples, dtype=jnp.int32)
    bin_index = first_bin + jnp.arange(nfreqs, dtype=jnp.int32)
    phase_turns = sample_index[:, None] * bin_index[None, :] % samples
    phase_angle = 2.0 * math.pi / samples * phase_turns.astype(jnp.float32)
    window = 0.5 - 0.5 * jnp.cos(2.0 * math.pi / samples * sample_index.astype(jnp.float32))
    weighting = (window / math.sqrt(samples))[:, None]
    stacked = jnp.stack([weighting * jnp.cos(phase_angle), -weighting * jnp.sin(phase_angle)], axis=2)
    return stacked.reshape(samples, 2 * nfreqs).astype(jnp.bfloat16)

def sphere_points(angles, radius, downward):
    polar_angle = angles[0]
    azimuth = angles[1]
    height = -jnp.cos(polar_angle) if downward else jnp.cos(polar_angle)
    return radius * jnp.stack([jnp.sin(polar_angle) * jnp.cos(azimuth), jnp.sin(polar_angle) * jnp.sin(azimuth), height])

def radiate(points, panel_pos, normals, wavenumbers, spectra, weighting):
    offset = points[:, :, None] - panel_pos[:, None, :]
    distance = jnp.sqrt(lax.optimization_barrier(jnp.sum(offset * offset, axis=0)))
    inverse = 1.0 / distance
    cosine = lax.optimization_barrier(jnp.sum(offset * normals[:, None, :], axis=0)) * inverse
    amplitude = RADIUS * weighting * inverse
    freq_count = wavenumbers.shape[0]
    per_freq = spectra.reshape(2, spectra.shape[1], freq_count, 2).transpose(2, 0, 1, 3)

    def one_freq(inputs):
        wavenumber, coeffs = inputs
        phase = wavenumber * distance
        cos_part = amplitude * jnp.cos(phase)
        sin_part = -amplitude * jnp.sin(phase)
        dip_real = cosine * (cos_part * inverse - wavenumber * sin_part)
        dip_imag = cosine * (sin_part * inverse + wavenumber * cos_part)
        mono_real = (-wavenumber * coeffs[0, :, 1])[None, :]
        mono_imag = (wavenumber * coeffs[0, :, 0])[None, :]
        load_real = coeffs[1, :, 0][None, :]
        load_imag = coeffs[1, :, 1][None, :]
        real_sum = lax.optimization_barrier(jnp.sum(cos_part * mono_real - sin_part * mono_imag + dip_real * load_real - dip_imag * load_imag, axis=1))
        imag_sum = lax.optimization_barrier(jnp.sum(cos_part * mono_imag + sin_part * mono_real + dip_real * load_imag + dip_imag * load_real, axis=1))
        return jnp.stack([real_sum, imag_sum], axis=1)
    result = lax.map(one_freq, (wavenumbers, per_freq))
    return result.transpose(1, 0, 2).reshape(points.shape[1], 2 * freq_count)

def layer_lengths(ray_count, ray_layer, ray_length):
    seg_rows = ray_layer.shape[0]
    segment = jnp.arange(seg_rows, dtype=jnp.int32)[:, None]
    used = jnp.where(segment < ray_count.reshape(1, -1), ray_length.reshape(seg_rows, -1), 0.0)
    layer_ids = jnp.arange(LAYERS, dtype=jnp.int32)[None, :, None]
    matches = ray_layer.reshape(seg_rows, 1, -1) == layer_ids
    return lax.optimization_barrier(jnp.sum(jnp.where(matches, used[:, None, :], 0.0), axis=0))

def ground_energy(power_rows, absorption, lengths, ray_weight, ray_ground, ground_count):
    optical_depth = jnp.dot(absorption, lengths, precision=lax.Precision.HIGHEST)
    freq_count = power_rows.shape[0]
    obs_count = power_rows.shape[1]
    shaped = optical_depth.reshape(freq_count, obs_count, RAYS)
    energy = power_rows[:, :, None] * ray_weight.reshape(1, obs_count, RAYS) * jnp.exp(-shaped)
    empty = jnp.zeros((freq_count, ground_count), jnp.float32)
    return empty.at[:, ray_ground.reshape(-1)].add(energy.reshape(freq_count, -1))

def reference(sources, panel_pos, normal_angles, observer_angles, absorption, ray_count, ray_layer, ray_length, ray_weight, ray_ground):
    transform_table = dft_table(SAMPLES, BIN0, FREQS)
    spectra = jnp.dot(sources.reshape(-1, SAMPLES), transform_table, preferred_element_type=jnp.float32)
    spectra = spectra.reshape(2, -1, 2 * FREQS)
    wavenumbers = (BIN0 + jnp.arange(FREQS, dtype=jnp.int32)).astype(jnp.float32) * (2.0 * math.pi / SAMPLES)
    points = sphere_points(observer_angles, RADIUS, True)
    normals = sphere_points(normal_angles, 1.0, False)
    weighting = GAIN / math.sqrt(PANELS)
    obs_spectrum = radiate(points, panel_pos, normals, wavenumbers, spectra, weighting)
    power_rows = (obs_spectrum[:, 0::2] * obs_spectrum[:, 0::2] + obs_spectrum[:, 1::2] * obs_spectrum[:, 1::2]).T
    lengths = layer_lengths(ray_count, ray_layer, ray_length)
    ground_power = ground_energy(power_rows, absorption, lengths, ray_weight, ray_ground, GROUND)
    return (obs_spectrum, ground_power)
```

```python
import functools
import math

import jax
import jax.numpy as jnp
import numpy as np
from jax import lax
from jax.experimental import pallas as pl
from jax.experimental.pallas import tpu as pltpu
from jax.sharding import PartitionSpec as P

SAMPLES = 1024
FREQS = 64
BIN0 = 32
RAYS = 64
LAYERS = 16
GROUND = 4096
RADIUS = 150.0
GAIN = 3.0
PANEL_SHARDS = 32
FREQ_SHARDS = 8
LOCAL = FREQS // FREQ_SHARDS
OBS_TILE = 256
ROWS = 16

F32 = jnp.float32
BF16 = jnp.bfloat16

SIN_HALF = (4.442882919124344, -7.308245686509013, 3.606354218431859, -0.8461116503677496, 0.10982451641401066)
COS_HALF = (1.4142134962552282, -6.978850948563772, 5.739460376906372, -1.883557905981734, 0.31068802751700825)
COS_STEP = (1.2110220208404683, -0.009766387925691403, -2.279682276148998e-05, 6.128264588074939e-08, 7.114804280952439e-11, -1.148571490941471e-13)
SIN_STEP = (0.7958368638857889, 0.0037153691223645335, -1.4981190780060094e-05, -2.3313394058735165e-08, 4.6755743732948126e-11, 4.3694425049187755e-14)


def horner(coeffs, x):
    value = x * coeffs[-1] + coeffs[-2]
    for c in coeffs[-3::-1]:
        value = value * x + c
    return value


def dft_rows():
    t = np.arange(SAMPLES)
    turns = (t[None, :] * (BIN0 + np.arange(FREQS))[:, None]) % SAMPLES
    angle = 2.0 * np.pi / SAMPLES * turns
    weighting = (0.5 - 0.5 * np.cos(2.0 * np.pi / SAMPLES * t)) / math.sqrt(SAMPLES)
    both = np.stack([weighting * np.cos(angle), -weighting * np.sin(angle)], axis=0)
    both = both.reshape(2, FREQ_SHARDS, LOCAL, SAMPLES).transpose(1, 0, 2, 3)
    return both.reshape(2 * FREQS, SAMPLES).astype(np.float32).astype(jnp.bfloat16)


def dft_kernel(table_ref, src_ref, out_ref):
    res = lax.dot_general(
        table_ref[...], src_ref[...], (((1,), (1,)), ((), ())), preferred_element_type=F32
    )
    for j in range(FREQ_SHARDS):
        base = 2 * LOCAL * j
        out_ref[j] = jnp.concatenate(
            [res[base : base + LOCAL], res[base + LOCAL : base + 2 * LOCAL]], axis=1
        )


def radiate_kernel(m0_ref, spec_ref, rows_ref, cols_ref, pts_ref, out_ref, w_ref):
    panels = cols_ref.shape[0]
    obs = pts_ref.shape[1]
    part = panels // FREQ_SHARDS
    m0 = m0_ref[0]
    turn_scale = m0 * (1.0 / SAMPLES)

    def whole(slot):
        return jnp.concatenate(
            [spec_ref[s][:, slot * part : (slot + 1) * part] for s in range(FREQ_SHARDS)], axis=1
        )

    q_re, l_re, q_im, l_im = (whole(slot) for slot in range(4))
    g_rows = rows_ref[0:8, :]
    h_rows = rows_ref[8:16, :]
    upper = lax.broadcasted_iota(jnp.int32, (8, panels), 0) < 4

    for f in range(LOCAL):
        k = (m0 + float(f)) * (2.0 * math.pi / SAMPLES)
        qr, qi, lr, li = (v[f : f + 1, :] for v in (q_re, q_im, l_re, l_im))
        qq = jnp.where(upper, -qi, qr)
        qq2 = jnp.where(upper, -qr, -qi)
        ll = jnp.where(upper, lr, li) * h_rows
        ll2 = jnp.where(upper, -li, lr) * h_rows
        kg = k * g_rows
        rows = [qq * kg + ll, qq2 * kg + ll2, k * ll2, -(k * ll)]
        for i, w in enumerate(rows):
            hi = w.astype(BF16)
            lo = (w - hi.astype(F32)).astype(BF16)
            both = jnp.concatenate([hi, lo], axis=0)
            for c in range(panels // 128):
                w_ref[f, c, :, i * 128 : (i + 1) * 128] = both[:, c * 128 : (c + 1) * 128]

    def tile(step, carry):
        start = pl.multiple_of(step * OBS_TILE, OBS_TILE)
        lanes = pl.ds(start, OBS_TILE)
        px = pts_ref[0:1, lanes]
        py = pts_ref[1:2, lanes]
        pz = pts_ref[2:3, lanes]
        sums = [None] * LOCAL
        for c in range(panels // 128):
            pieces = [[[] for _ in range(4)] for _ in range(LOCAL)]
            for s in range(128 // ROWS):
                at = c * 128 + s * ROWS
                cx = cols_ref[at : at + ROWS, 0:1]
                cy = cols_ref[at : at + ROWS, 1:2]
                cz = cols_ref[at : at + ROWS, 2:3]
                c2 = cols_ref[at : at + ROWS, 3:4]
                r2 = c2 + (cx * px + cy * py + cz * pz)
                inv = lax.rsqrt(r2)
                r = r2 * inv
                t = r * turn_scale
                t = t - ((t + 12582912.0) - 12582912.0)
                u = t * t
                sn = t * horner(SIN_HALF, u)
                cs = horner(COS_HALF, u)
                inv3 = inv * inv * inv
                a0 = inv3 - inv3 * (sn * sn)
                b0 = -(inv3 * (sn * cs))
                y = r - RADIUS
                two_cos = horner(COS_STEP, y)
                sin1 = horner(SIN_STEP, y)
                cos1 = 0.5 * two_cos
                a1 = a0 * cos1 + b0 * sin1
                b1 = b0 * cos1 - a0 * sin1
                for f in range(LOCAL):
                    pieces[f][0].append(a0.astype(BF16))
                    pieces[f][1].append(b0.astype(BF16))
                    pieces[f][2].append((a0 * r).astype(BF16))
                    pieces[f][3].append((b0 * r).astype(BF16))
                    if f < LOCAL - 1:
                        if f < LOCAL - 2:
                            a2 = two_cos * a1 - a0
                            b2 = two_cos * b1 - b0
                        a0, b0 = a1, b1
                        if f < LOCAL - 2:
                            a1, b1 = a2, b2
            for f in range(LOCAL):
                fn = jnp.concatenate(sum(pieces[f], []), axis=0)
                got = jnp.dot(w_ref[f, c], fn, preferred_element_type=F32)
                sums[f] = got if sums[f] is None else sums[f] + got
        ones = jnp.ones((1, OBS_TILE), F32)
        mix = jnp.concatenate([ones, px, py, pz, ones, px, py, pz], axis=0)
        res, ims = [], []
        for f in range(LOCAL):
            v = (sums[f][0:8] + sums[f][8:16]) * mix
            res.append(jnp.sum(v[0:4], axis=0, keepdims=True))
            ims.append(jnp.sum(v[4:8], axis=0, keepdims=True))
        re = jnp.concatenate(res, axis=0)
        im = jnp.concatenate(ims, axis=0)
        for b in range(OBS_TILE // RAYS):
            out_ref[step * (OBS_TILE // RAYS) + b] = jnp.concatenate(
                [re[:, b * RAYS : (b + 1) * RAYS], im[:, b * RAYS : (b + 1) * RAYS]], axis=1
            )
        return carry

    lax.fori_loop(0, obs // OBS_TILE, tile, 0)


def rays_kernel(absorb_ref, count_ref, layer_ref, length_ref, weight_ref, ground_ref, gain_ref, low_ref):
    segs, rows = layer_ref.shape
    tile = 1024
    for q in range(rows // tile):
        lanes = slice(q * tile, (q + 1) * tile)
        count = count_ref[0:1, lanes]
        ids = lax.broadcasted_iota(jnp.int32, (LAYERS, tile), 0)
        lengths = jnp.zeros((LAYERS, tile), F32)
        for s in range(segs):
            used = jnp.where(count > s, length_ref[s : s + 1, lanes], 0.0)
            lengths = lengths + jnp.where(layer_ref[s : s + 1, lanes] == ids, used, 0.0)
        depth = jnp.dot(
            absorb_ref[...], lengths, preferred_element_type=F32, precision=lax.Precision.HIGHEST
        )
        gain_ref[:, lanes] = weight_ref[0:1, lanes] * jnp.exp(-depth)
        low = ground_ref[0:1, lanes] & 127
        spots = lax.broadcasted_iota(jnp.int32, (128, tile), 0)
        low_ref[:, lanes] = jnp.where(low == spots, 1.0, 0.0).astype(BF16)


def ground_kernel(recv_ref, gain_ref, low_ref, ground_ref, spec_ref, out_ref, z_ref):
    total = jnp.sum(recv_ref[...], axis=0) * (RADIUS * GAIN / math.sqrt(8192))
    spec_ref[...] = total
    sq = total * total
    power = sq[:, 0:RAYS] + sq[:, RAYS : 2 * RAYS]
    rows = gain_ref.shape[1]
    left = lax.broadcasted_iota(jnp.int32, (LOCAL, 128), 1) < 64
    for q in range(rows // 128):
        lanes = slice(q * 128, (q + 1) * 128)
        p = jnp.where(left, power[:, 2 * q : 2 * q + 1], power[:, 2 * q + 1 : 2 * q + 2])
        e = p * gain_ref[:, lanes]
        high = lax.shift_right_logical(ground_ref[0:1, lanes], 7)
        hi = e.astype(BF16).astype(F32)
        lo = e - hi
        both = jnp.concatenate([hi, lo], axis=0)
        for h in range(GROUND // 128):
            z_ref[h * 16 : (h + 1) * 16, lanes] = jnp.where(high == h, both, 0.0).astype(BF16)
    res = lax.dot_general(
        z_ref[...], low_ref[...], (((1,), (1,)), ((), ())), preferred_element_type=F32
    )
    for h in range(GROUND // 128):
        out_ref[h] = res[h * 16 : h * 16 + 8] + res[h * 16 + 8 : h * 16 + 16]


def vmem(n):
    return [pl.BlockSpec(memory_space=pltpu.VMEM)] * n


def params(mb):
    return pltpu.CompilerParams(vmem_limit_bytes=mb * 1024 * 1024)


def shards(
    sources,
    panel_pos,
    normal_angles,
    observer_angles,
    absorption,
    ray_count,
    ray_layer,
    ray_length,
    ray_weight,
    ray_ground,
):
    panels = panel_pos.shape[1]
    obs = observer_angles.shape[1]
    rays = ray_count.shape[0]
    part = sources.shape[1]
    fi = lax.axis_index("freq")

    with jax.named_scope("dft"):
        table = jnp.asarray(dft_rows())
        partial = pl.pallas_call(
            dft_kernel,
            out_shape=jax.ShapeDtypeStruct((FREQ_SHARDS, LOCAL, 4 * part), F32),
            in_specs=vmem(2),
            out_specs=vmem(1)[0],
            compiler_params=params(16),
            name="dft",
        )(table, sources.reshape(2 * part, SAMPLES))
    with jax.named_scope("bins_to_owners"):
        spec = lax.all_to_all(partial, "freq", 0, 0, tiled=True)

    with jax.named_scope("geometry_rows"):
        st, ct = jnp.sin(observer_angles[0]), jnp.cos(observer_angles[0])
        sp, cp = jnp.sin(observer_angles[1]), jnp.cos(observer_angles[1])
        points = RADIUS * jnp.stack([st * cp, st * sp, -ct])
        nt, mt = jnp.sin(normal_angles[0]), jnp.cos(normal_angles[0])
        np_, mp = jnp.sin(normal_angles[1]), jnp.cos(normal_angles[1])
        normals = jnp.stack([nt * mp, nt * np_, mt])
        size2 = RADIUS * RADIUS + jnp.sum(panel_pos * panel_pos, axis=0, keepdims=True)
        g_rows = jnp.concatenate([size2, -2.0 * panel_pos], axis=0)
        h_rows = jnp.concatenate(
            [-jnp.sum(normals * panel_pos, axis=0, keepdims=True), normals], axis=0
        )
        rows = jnp.concatenate([g_rows, g_rows, h_rows, h_rows], axis=0)
        cols = jnp.concatenate([-2.0 * panel_pos, size2], axis=0).T
        m0 = (BIN0 + LOCAL * fi).astype(F32).reshape(1)

    with jax.named_scope("radiate"):
        partial_obs = pl.pallas_call(
            radiate_kernel,
            out_shape=jax.ShapeDtypeStruct((obs // RAYS, LOCAL, 2 * RAYS), F32),
            in_specs=[pl.BlockSpec(memory_space=pltpu.SMEM)] + vmem(4),
            out_specs=vmem(1)[0],
            scratch_shapes=[pltpu.VMEM((LOCAL, panels // 128, 16, 512), BF16)],
            compiler_params=params(48),
            cost_estimate=pl.CostEstimate(flops=10**9, bytes_accessed=10**6, transcendentals=0),
            name="radiate",
        )(m0, spec, rows, cols, points)
    with jax.named_scope("observers_to_owners"):
        recv = lax.all_to_all(partial_obs, "panel", 0, 0, tiled=True)

    with jax.named_scope("rays"):
        own = lax.dynamic_slice_in_dim(absorption, fi * LOCAL, LOCAL, axis=0)
        ground_row = ray_ground.reshape(1, rays)
        gain, low = pl.pallas_call(
            rays_kernel,
            out_shape=(
                jax.ShapeDtypeStruct((LOCAL, rays), F32),
                jax.ShapeDtypeStruct((128, rays), BF16),
            ),
            in_specs=vmem(6),
            out_specs=tuple(vmem(2)),
            compiler_params=params(32),
            cost_estimate=pl.CostEstimate(flops=10**7, bytes_accessed=10**6, transcendentals=0),
            name="rays",
        )(
            own,
            ray_count.reshape(1, rays),
            ray_layer,
            ray_length,
            ray_weight.reshape(1, rays),
            ground_row,
        )

    with jax.named_scope("ground"):
        spectrum, ground_part = pl.pallas_call(
            ground_kernel,
            out_shape=(
                jax.ShapeDtypeStruct((LOCAL, 2 * RAYS), F32),
                jax.ShapeDtypeStruct((PANEL_SHARDS, LOCAL, GROUND // PANEL_SHARDS), F32),
            ),
            in_specs=vmem(4),
            out_specs=tuple(vmem(2)),
            scratch_shapes=[pltpu.VMEM((GROUND // 128 * 16, rays), BF16)],
            compiler_params=params(40),
            name="ground",
        )(recv, gain, low, ground_row)
    obs_spectrum = (
        spectrum.reshape(LOCAL, 2, RAYS).transpose(2, 0, 1).reshape(RAYS, 2 * LOCAL)
    )
    with jax.named_scope("ground_to_owners"):
        mine = jnp.sum(lax.all_to_all(ground_part, "panel", 0, 0, tiled=True), axis=0)
    with jax.named_scope("all_bins"):
        copies = jnp.broadcast_to(mine[None], (FREQ_SHARDS,) + mine.shape)
        ground_power = lax.all_to_all(copies, "freq", 0, 0, tiled=True)
    return (obs_spectrum, ground_power.reshape(FREQS, GROUND // PANEL_SHARDS))


def solution(mesh):
    return jax.shard_map(
        shards,
        mesh=mesh,
        in_specs=(
            P(None, ("panel", "freq"), None),
            P(None, "panel"),
            P(None, "panel"),
            P(),
            P(),
            P("panel"),
            P(None, "panel"),
            P(None, "panel"),
            P("panel"),
            P("panel"),
        ),
        out_specs=(P("panel", "freq"), P(None, "panel")),
        check_vma=False,
    )
```

```python
import math

import jax
import jax.numpy as jnp
import numpy as np
from jax import lax
from jax.experimental import pallas as pl
from jax.experimental.pallas import tpu as pltpu
from jax.sharding import PartitionSpec as P

SAMPLES = 1024
FREQS = 64
BIN0 = 32
RAYS = 64
LAYERS = 16
GROUND = 4096
RADIUS = 150.0
GAIN = 3.0
PANELS = 8192
SHARDS = 32
GROUPS = 8
CHIPS = SHARDS * GROUPS // 2
BINS = FREQS // 2
OWN = PANELS // (SHARDS * GROUPS)
PAIR = 2 * OWN
OBS_TILE = 512
ROWS = 16

F32 = jnp.float32
BF16 = jnp.bfloat16

SIN_HALF = (4.442882919124344, -7.308245686509013, 3.606354218431859, -0.8461116503677496, 0.10982451641401066)
COS_HALF = (1.4142134962552282, -6.978850948563772, 5.739460376906372, -1.883557905981734, 0.31068802751700825)
COS_STEP = (
    -0.53342551167462, -0.023654623427363474, 4.016642697431393e-05, 5.937236542349045e-07,
    -5.040166110800607e-10, -4.470245655063533e-12, 2.492488156438906e-15, 1.5819745095405966e-17,
)
SIN_STEP = (
    0.9637760598779563, -0.0032730579567440193, -7.257140853115864e-05, 8.21527316453533e-08,
    9.10641004058044e-10, -6.185417897022673e-13, -4.503347445205572e-15, 2.188956532785521e-18,
)


def horner(coeffs, x):
    value = x * coeffs[-1] + coeffs[-2]
    for c in coeffs[-3::-1]:
        value = value * x + c
    return value


def sin_cos(angle):
    return turn_sin_cos(angle * (0.5 / math.pi))


def turn_sin_cos(t):
    u = t * t
    s = t * horner(SIN_HALF, u)
    return s * horner(COS_HALF, u), 1.0 - s * s


def own_place():
    return lax.rem(lax.axis_index("panel"), 2), lax.axis_index("freq")


def near(turns):
    return turns - ((turns + 12582912.0) - 12582912.0)


def spectra_of(table, series):
    return lax.dot_general(
        table, series.reshape(PAIR, SAMPLES), (((1,), (1,)), ((), ())), preferred_element_type=F32
    )


def place_of(pos, ang):
    width = pos.shape[1]
    place = jnp.concatenate([pos, ang, jnp.zeros((3, width), F32)], axis=0)
    shift = lax.rem(width - OWN * own_place()[1], width)
    return pltpu.roll(place, shift, 1)[:, 0:PAIR]


def prepare_kernel(src_ref, pos_ref, ang_ref, obs_ref, keep_ref, send_ref, pts_ref, src, pos, ang, obs, sems):
    copies = [
        pltpu.make_async_copy(a, b, sems.at[i])
        for i, (a, b) in enumerate(
            [(obs_ref, obs), (src_ref.at[0], src.at[0]), (src_ref.at[1], src.at[1]), (pos_ref, pos), (ang_ref, ang)]
        )
    ]
    for copy in copies:
        copy.start()

    sample = lax.broadcasted_iota(jnp.int32, (1, SAMPLES), 1).astype(F32)
    window = (0.5 - 0.5 * turn_sin_cos(near(sample * (1.0 / SAMPLES)))[1]) * (1.0 / math.sqrt(SAMPLES))
    bins = lax.broadcasted_iota(jnp.int32, (BINS, SAMPLES), 0).astype(F32)
    tables = []
    for parity in range(2):
        turns = ((2.0 * bins + float(BIN0 + parity)) * sample) * (1.0 / SAMPLES)
        sn, cs = turn_sin_cos(near(turns))
        tables.append(jnp.concatenate([window * cs, -(window * sn)], axis=0).astype(BF16))

    copies[0].wait()
    s, c = sin_cos(obs[...])
    pts_ref[0:1] = RADIUS * s[0:1] * c[1:2]
    pts_ref[1:2] = RADIUS * s[0:1] * s[1:2]
    pts_ref[2:3] = -RADIUS * c[0:1]

    for copy in copies[1:]:
        copy.wait()
    low, high = (spectra_of(table, src[...]) for table in tables)
    first = own_place()[0] == 0
    keep_ref[0:FREQS] = jnp.where(first, low, high)
    send_ref[0:FREQS] = jnp.where(first, high, low)
    place = place_of(pos[...], ang[...])
    keep_ref[FREQS : FREQS + 8] = place
    send_ref[FREQS : FREQS + 8] = place


def radiate_kernel(
    mine_ref, other_ref, pts_ref, out_ref, w_ref, cols_ref, fa_ref, fb_ref, block, sems
):
    m0 = BIN0 + own_place()[0].astype(F32)
    turn_scale = m0 * (1.0 / SAMPLES)
    tiles = pts_ref.shape[1] // OBS_TILE

    def lanes_of(rows, at):
        a, b = mine_ref[rows, at : at + OWN], other_ref[rows, at : at + OWN]
        return jnp.concatenate([a, b, a, b], axis=1)

    place = lanes_of(slice(FREQS, FREQS + 8), 0)
    pos = [place[d : d + 1] for d in range(3)]
    s, c = sin_cos(place[3:5])
    normal = [s[0:1] * c[1:2], s[0:1] * s[1:2], c[0:1]]
    size2 = RADIUS * RADIUS + (pos[0] * pos[0] + pos[1] * pos[1] + pos[2] * pos[2])
    facing = pos[0] * normal[0] + pos[1] * normal[1] + pos[2] * normal[2]
    back = [-2.0 * v for v in pos]
    cols_ref[...] = jnp.concatenate(back + [size2] * 5, axis=0).T

    def doubled(first, rest):
        return jnp.concatenate([v for v in [first] + rest for _ in range(2)], axis=0)

    shape = (8, 2 * PAIR)
    odd = (lax.broadcasted_iota(jnp.int32, shape, 0) & 1) == 1
    right = lax.broadcasted_iota(jnp.int32, shape, 1) >= PAIR
    same = odd == right
    sign_a = jnp.where(odd & ~right, 1.0, -1.0)
    sign_b = jnp.where(right & ~odd, -1.0, 1.0)
    g = doubled(size2, back) * sign_a
    h = doubled(-facing, normal)
    h_a, h_b = h * sign_a, h * sign_b
    q = lanes_of(slice(0, FREQS), 0)
    ld = lanes_of(slice(0, FREQS), OWN)
    for n in range(BINS):
        k = (m0 + 2.0 * n) * (2.0 * math.pi / SAMPLES)
        qr, qi = q[n : n + 1], q[BINS + n : BINS + n + 1]
        lr, li = ld[n : n + 1], ld[BINS + n : BINS + n + 1]
        turned = jnp.where(same, li, lr)
        w0 = k * (jnp.where(same, qi, qr) * g) + jnp.where(same, lr, li) * h_b
        w1 = k * (turned * h_a)
        for i, w in enumerate((w0, w1)):
            hi = w.astype(BF16)
            lo = (w - hi.astype(F32)).astype(BF16)
            w_ref[n, :, i * 128 : (i + 1) * 128] = jnp.concatenate([hi, lo], axis=0)

    def point_rows(t):
        lanes = slice(t * OBS_TILE, (t + 1) * OBS_TILE)
        return [pts_ref[d : d + 1, lanes] for d in range(3)]

    def functions(t, f_ref, s):
        px, py, pz = point_rows(t)
        at = s * ROWS
        cx, cy, cz, c2 = (cols_ref[at : at + ROWS, d : d + 1] for d in range(4))
        r2 = c2 + (cx * px + cy * py + cz * pz)
        inv = lax.rsqrt(r2)
        r = r2 * inv
        turns = near(r * turn_scale)
        u = turns * turns
        sn = turns * horner(SIN_HALF, u)
        cs = horner(COS_HALF, u)
        inv3 = inv * inv * inv
        a0 = inv3 - inv3 * (sn * sn)
        b0 = -(inv3 * (sn * cs))
        y = r - RADIUS
        two_cos = horner(COS_STEP, y)
        sin1 = horner(SIN_STEP, y)
        cos1 = 0.5 * two_cos
        a1 = a0 * cos1 + b0 * sin1
        b1 = b0 * cos1 - a0 * sin1
        for n in range(BINS):
            for i, v in enumerate((a0, b0, a0 * r, b0 * r)):
                f_ref[n, i * PAIR + at : i * PAIR + at + ROWS, :] = v.astype(BF16)
            if n < BINS - 2:
                a0, b0, a1, b1 = a1, b1, two_cos * a1 - a0, two_cos * b1 - b0
            else:
                a0, b0 = a1, b1

    upper = lax.broadcasted_iota(jnp.int32, (8, OBS_TILE), 0) < 4
    inner = (lax.broadcasted_iota(jnp.int32, (8, OBS_TILE), 0) & 2) == 0
    blocks = OBS_TILE // 128

    def sums(t, f_ref, part, mix):
        outs = []
        for j in (2 * part, 2 * part + 1):
            got = []
            for i in range(4):
                acc = jnp.dot(w_ref[4 * j + i], f_ref[4 * j + i], preferred_element_type=F32)
                v = (acc[0:8] + acc[8:16]) * mix
                got.append(v + pltpu.roll(v, 4, 0))
            ab = jnp.where(upper, got[0], got[2])
            cd = jnp.where(upper, got[1], got[3])
            outs.append(jnp.where(inner, ab + pltpu.roll(ab, 6, 0), cd + pltpu.roll(cd, 2, 0)))
        both = jnp.concatenate(outs, axis=0).astype(BF16)
        for b in range(blocks):
            block[t, b, part * 16 : part * 16 + 16] = both[:, b * 128 : (b + 1) * 128]

    def mix_of(t):
        px, py, pz = point_rows(t)
        ones = jnp.ones((1, OBS_TILE), F32)
        return jnp.concatenate([ones, ones, px, px, py, py, pz, pz], axis=0)

    copies = []

    def send(t):
        copy = pltpu.make_async_copy(block.at[t], out_ref.at[pl.ds(t * blocks, blocks)], sems.at[t])
        copy.start()
        copies.append(copy)

    scratch = (fa_ref, fb_ref)
    steps = PAIR // ROWS
    for part in range(steps):
        functions(0, fa_ref, part)
    for t in range(tiles):
        mix = mix_of(t)
        for part in range(steps):
            sums(t, scratch[t % 2], part, mix)
            if t + 1 < tiles:
                functions(t + 1, scratch[(t + 1) % 2], part)
        send(t)
    for copy in copies:
        copy.wait()


def rays_kernel(absorb_ref, count_ref, layer_ref, length_ref, weight_ref, ground_ref, keep_ref, send_ref):
    core, group = own_place()
    own = absorb_ref[pl.ds(pl.multiple_of(group * 8, 8), 8), :]
    even = [own[2 * i : 2 * i + 1] for i in range(4)]
    odds = [own[2 * i + 1 : 2 * i + 2] for i in range(4)]
    first = core == 0
    rows8 = jnp.concatenate(
        [jnp.where(first, a, b) for a, b in zip(even, odds)]
        + [jnp.where(first, b, a) for a, b in zip(even, odds)],
        axis=0,
    )
    segs, rows = layer_ref.shape
    tile = 1024
    for q in range(rows // tile):
        lanes = slice(q * tile, (q + 1) * tile)
        count = count_ref[0:1, lanes]
        ids = lax.broadcasted_iota(jnp.int32, (LAYERS, tile), 0)
        lengths = jnp.zeros((LAYERS, tile), F32)
        for s in range(segs):
            used = jnp.where(count > s, length_ref[s : s + 1, lanes], 0.0)
            lengths = lengths + jnp.where(layer_ref[s : s + 1, lanes] == ids, used, 0.0)
        depth = jnp.dot(rows8, lengths, preferred_element_type=F32, precision=lax.Precision.HIGHEST)
        gain = weight_ref[0:1, lanes] * jnp.exp(-depth)
        ground = jnp.broadcast_to(ground_ref[0:1, lanes].astype(F32), (4, tile))
        keep_ref[:, lanes] = jnp.concatenate([gain[0:4], ground], axis=0)
        send_ref[:, lanes] = jnp.concatenate([gain[4:8], ground], axis=0)


def spots_kernel(mine_ref, other_ref, gain_ref, high_ref, low_ref):
    rows = mine_ref.shape[1]
    half = lax.shift_right_logical(lax.broadcasted_iota(jnp.int32, (8, 128), 0), 2)
    spots = lax.broadcasted_iota(jnp.int32, (128, 128), 1)
    for side, ref in enumerate((mine_ref, other_ref)):
        for q in range(rows // 128):
            block = ref[:, q * 128 : (q + 1) * 128]
            at = slice(side * rows + q * 128, side * rows + (q + 1) * 128)
            gain_ref[:, at] = jnp.concatenate([block[0:4], block[0:4]], axis=0)
            ground = jnp.concatenate([block[4:8], block[4:8]], axis=0).astype(jnp.int32)
            high = (lax.shift_right_logical(ground, 7) - half).astype(F32)
            high_ref[:, at] = jnp.concatenate([high, high], axis=0).astype(BF16)
            low = (ground & 127).astype(F32).T.astype(jnp.int32)
            low_ref[at, :] = jnp.where(low[:, 0:1] == spots, 1.0, 0.0).astype(BF16)


def ground_kernel(recv_ref, gain_ref, high_ref, low_ref, spec_ref, out_ref, z_ref, both_ref, sems):
    total = recv_ref[0].astype(F32)
    for d in range(1, recv_ref.shape[0]):
        total = total + recv_ref[d].astype(F32)
    total = (total[0:8] + total[8:16]) * (RADIUS * GAIN / math.sqrt(PANELS))
    first = own_place()[0] == 0
    turned = pltpu.roll(total, RAYS, 1)
    total = jnp.where(first, total, turned)
    spec_ref[...] = total
    sq = total * total
    power = jnp.concatenate([sq[2 * i : 2 * i + 1] + sq[2 * i + 1 : 2 * i + 2] for i in range(4)] * 2, axis=0)
    left = lax.broadcasted_iota(jnp.int32, (8, 128), 1) < RAYS
    nothing = jnp.zeros((16, 128), BF16)
    rows = gain_ref.shape[1]
    cut = 1024
    res = None
    for k in range(rows // cut):
        for q in range(k * cut // 128, (k + 1) * cut // 128):
            at = slice(q * 128, (q + 1) * 128)
            p = jnp.where(left, power[:, 2 * q : 2 * q + 1], power[:, 2 * q + 1 : 2 * q + 2])
            e = p * gain_ref[:, at]
            hi = e.astype(BF16).astype(F32)
            both = jnp.concatenate([hi, e - hi], axis=0).astype(BF16)
            high = high_ref[:, at]
            for b in range(GROUND // 256):
                z_ref[b * 16 : (b + 1) * 16, at] = jnp.where(high == float(2 * b), both, nothing)
        ks = slice(k * cut, (k + 1) * cut)
        got = jnp.dot(z_ref[:, ks], low_ref[ks, :], preferred_element_type=F32)
        res = got if res is None else res + got
    for b in range(GROUND // 256):
        v = res[b * 16 : b * 16 + 8] + res[b * 16 + 8 : b * 16 + 16]
        both_ref[b] = jnp.concatenate([v, v], axis=0).astype(BF16)
    copies = [
        pltpu.make_async_copy(both_ref, out_ref.at[:, pl.ds(j * 16, 16)], sems.at[j]) for j in range(GROUPS // 2)
    ]
    for copy in copies:
        copy.start()
    for copy in copies:
        copy.wait()


def owners_kernel(recv_ref, keep_ref, send_ref):
    first = own_place()[0] == 0
    for pair in range(GROUPS // 2):
        total = recv_ref[pair].astype(F32)
        for b in range(1, GROUND // 256):
            total = total + recv_ref[b * (GROUPS // 2) + pair].astype(F32)
        for i in range(2):
            low, high = total[i * 8 : i * 8 + 4], total[i * 8 + 4 : i * 8 + 8]
            at = (2 * pair + i) * 4
            keep_ref[at : at + 4] = jnp.where(first, low, high)
            send_ref[at : at + 4] = jnp.where(first, high, low)


def finish_kernel(keep_ref, other_ref, out_ref):
    first = own_place()[0] == 0
    keep, other = keep_ref[...], other_ref[...]
    out_ref[pl.ds(0, BINS, stride=2), :] = jnp.where(first, keep, other)
    out_ref[pl.ds(1, BINS, stride=2), :] = jnp.where(first, other, keep)


def call(body, out, scratch=(), vm=32, flops=10**6, name=None, far=(), far_out=()):
    def run(*args):
        def spec(i, places):
            return pl.BlockSpec(memory_space=pl.ANY if i in places else pltpu.VMEM)

        return pl.pallas_call(
            body,
            out_shape=out,
            in_specs=[spec(i, far) for i in range(len(args))],
            out_specs=tuple(spec(i, far_out) for i in range(len(out))),
            scratch_shapes=list(scratch),
            compiler_params=pltpu.CompilerParams(vmem_limit_bytes=vm * 1024 * 1024),
            cost_estimate=pl.CostEstimate(flops=flops, bytes_accessed=10**6, transcendentals=0),
            name=name,
        )(*args)

    return run


def struct(*shape, dtype=F32):
    return jax.ShapeDtypeStruct(shape, dtype)


def swap(value):
    return lax.ppermute(value, "panel", [(i, i ^ 1) for i in range(SHARDS)])


def between_chips(value):
    groups = [
        [(2 * b + c) * GROUPS + j for b in range(SHARDS // 2) for j in range(GROUPS)] for c in range(2)
    ]
    value = value.reshape(CHIPS, 8, 128)
    return lax.all_to_all(
        value, ("panel", "freq"), 0, 0, axis_index_groups=groups, tiled=True
    ).reshape(CHIPS // 2, 16, 128)


def shards(
    sources,
    panel_pos,
    normal_angles,
    observer_angles,
    absorption,
    ray_count,
    ray_layer,
    ray_length,
    ray_weight,
    ray_ground,
):
    obs = observer_angles.shape[1]
    rays = ray_count.shape[0]
    core = lax.rem(lax.axis_index("panel"), 2)

    with jax.named_scope("prepare"):
        keep, send, points = call(
            prepare_kernel,
            (pltpu.VMEM((FREQS + 8, PAIR), F32), pltpu.VMEM((FREQS + 8, PAIR), F32), pltpu.VMEM((8, obs), F32)),
            scratch=[
                pltpu.VMEM(sources.shape, BF16),
                pltpu.VMEM(panel_pos.shape, F32),
                pltpu.VMEM(normal_angles.shape, F32),
                pltpu.VMEM(observer_angles.shape, F32),
                pltpu.SemaphoreType.DMA((5,)),
            ],
            vm=58,
            flops=10**7,
            name="prepare",
            far=(0, 1, 2, 3),
        )(sources, panel_pos, normal_angles, observer_angles)
        other = swap(send)
    with jax.named_scope("rays"):
        gain, gain_send = call(rays_kernel, (struct(8, rays),) * 2, flops=10**7, name="rays")(
            absorption,
            ray_count.reshape(1, rays),
            ray_layer,
            ray_length,
            ray_weight.reshape(1, rays),
            ray_ground.reshape(1, rays),
        )
        gain_other = swap(gain_send)
    with jax.named_scope("radiate"):
        (partial_obs,) = call(
            radiate_kernel,
            (struct(obs // 128, FREQS, 128, dtype=BF16),),
            scratch=[
                pltpu.VMEM((BINS, 16, 4 * PAIR), BF16),
                pltpu.VMEM((2 * PAIR, 8), F32),
                pltpu.VMEM((BINS, 4 * PAIR, OBS_TILE), BF16),
                pltpu.VMEM((BINS, 4 * PAIR, OBS_TILE), BF16),
                pltpu.VMEM((obs // OBS_TILE, OBS_TILE // 128, FREQS, 128), BF16),
                pltpu.SemaphoreType.DMA((obs // OBS_TILE,)),
            ],
            vm=40,
            flops=10**9,
            name="radiate",
            far_out=(0,),
        )(keep, other, points)
    with jax.named_scope("observers_to_owners"):
        recv = between_chips(partial_obs)
    with jax.named_scope("spots"):
        spots = call(
            spots_kernel,
            (struct(8, 2 * rays), struct(16, 2 * rays, dtype=BF16), struct(2 * rays, 128, dtype=BF16)),
            flops=10**7,
            name="spots",
        )(gain, gain_other)
    with jax.named_scope("ground"):
        spectrum, ground_part = call(
            ground_kernel,
            (struct(8, 128), struct(GROUND // 256, FREQS, 128, dtype=BF16)),
            scratch=[
                pltpu.VMEM((256, 2 * rays), BF16),
                pltpu.VMEM((GROUND // 256, 16, 128), BF16),
                pltpu.SemaphoreType.DMA((GROUPS // 2,)),
            ],
            name="ground",
            far_out=(1,),
        )(recv, *spots)
    with jax.named_scope("ground_to_owners"):
        got = between_chips(ground_part)
        keep, send = call(owners_kernel, (struct(BINS, 128),) * 2, name="owners")(got)
        other = swap(send)
        (ground_power,) = call(finish_kernel, (struct(FREQS, 128),), name="finish")(keep, other)
    with jax.named_scope("spectrum"):
        mine = spectrum[:, 0:RAYS]
        other = swap(spectrum[:, RAYS:])
        even = jnp.where(core == 0, mine, other).reshape(4, 2, RAYS)
        odds = jnp.where(core == 0, other, mine).reshape(4, 2, RAYS)
        obs_spectrum = jnp.stack([even, odds], axis=1).reshape(16, RAYS).T
    return (obs_spectrum, ground_power)


def solution(mesh):
    return jax.shard_map(
        shards,
        mesh=mesh,
        in_specs=(
            P(None, ("panel", "freq"), None),
            P(None, "panel"),
            P(None, "panel"),
            P(),
            P(),
            P("panel"),
            P(None, "panel"),
            P(None, "panel"),
            P("panel"),
            P("panel"),
        ),
        out_specs=(P("panel", "freq"), P(None, "panel")),
        check_vma=False,
    )
```

```python
import math

import jax
import jax.numpy as jnp
import numpy as np
from jax import lax
from jax.experimental import pallas as pl
from jax.experimental.pallas import tpu as pltpu
from jax.sharding import PartitionSpec as P

SAMPLES = 1024
FREQS = 64
BIN0 = 32
RAYS = 64
LAYERS = 16
GROUND = 4096
RADIUS = 150.0
GAIN = 3.0
PANELS = 8192
SHARDS = 32
GROUPS = 8
CHIPS = SHARDS * GROUPS // 2
BINS = FREQS // 2
OWN = PANELS // (SHARDS * GROUPS)
PAIR = 2 * OWN
OBS_TILE = 256
FN_LANES = 256
ROWS = 16

F32 = jnp.float32
BF16 = jnp.bfloat16

SIN_HALF = (4.442882919124344, -7.308245686509013, 3.606354218431859, -0.8461116503677496, 0.10982451641401066)
COS_HALF = (1.4142134962552282, -6.978850948563772, 5.739460376906372, -1.883557905981734, 0.31068802751700825)
COS_STEP = (
    -0.53342551167462, -0.023654623427363474, 4.016642697431393e-05, 5.937236542349045e-07,
    -5.040166110800607e-10, -4.470245655063533e-12, 2.492488156438906e-15, 1.5819745095405966e-17,
)
SIN_STEP = (
    0.9637760598779563, -0.0032730579567440193, -7.257140853115864e-05, 8.21527316453533e-08,
    9.10641004058044e-10, -6.185417897022673e-13, -4.503347445205572e-15, 2.188956532785521e-18,
)


def horner(coeffs, x):
    value = x * coeffs[-1] + coeffs[-2]
    for c in coeffs[-3::-1]:
        value = value * x + c
    return value


def sin_cos(angle):
    return turn_sin_cos(angle * (0.5 / math.pi))


def turn_sin_cos(t):
    u = t * t
    s = t * horner(SIN_HALF, u)
    return s * horner(COS_HALF, u), 1.0 - s * s


def own_place():
    return lax.rem(lax.axis_index("panel"), 2), lax.axis_index("freq")


def near(turns):
    return turns - ((turns + 12582912.0) - 12582912.0)


def spectra_of(table, series):
    return lax.dot_general(
        table, series.reshape(PAIR, SAMPLES), (((1,), (1,)), ((), ())), preferred_element_type=F32
    )


def place_of(pos, ang):
    width = pos.shape[1]
    place = jnp.concatenate([pos, ang, jnp.zeros((3, width), F32)], axis=0)
    shift = lax.rem(width - OWN * own_place()[1], width)
    return pltpu.roll(place, shift, 1)[:, 0:PAIR]


def prepare_kernel(src_ref, pos_ref, ang_ref, obs_ref, keep_ref, send_ref, pts_ref, src, pos, ang, obs, sems):
    copies = [
        pltpu.make_async_copy(a, b, sems.at[i])
        for i, (a, b) in enumerate(
            [(obs_ref, obs), (src_ref.at[0], src.at[0]), (src_ref.at[1], src.at[1]), (pos_ref, pos), (ang_ref, ang)]
        )
    ]
    for copy in copies:
        copy.start()

    sample = lax.broadcasted_iota(jnp.int32, (1, SAMPLES), 1).astype(F32)
    window = (0.5 - 0.5 * turn_sin_cos(near(sample * (1.0 / SAMPLES)))[1]) * (1.0 / math.sqrt(SAMPLES))
    bins = lax.broadcasted_iota(jnp.int32, (BINS, SAMPLES), 0).astype(F32)
    tables = []
    for parity in range(2):
        turns = ((2.0 * bins + float(BIN0 + parity)) * sample) * (1.0 / SAMPLES)
        sn, cs = turn_sin_cos(near(turns))
        tables.append(jnp.concatenate([window * cs, -(window * sn)], axis=0).astype(BF16))

    copies[0].wait()
    s, c = sin_cos(obs[...])
    pts_ref[0:1] = RADIUS * s[0:1] * c[1:2]
    pts_ref[1:2] = RADIUS * s[0:1] * s[1:2]
    pts_ref[2:3] = -RADIUS * c[0:1]

    for copy in copies[1:]:
        copy.wait()
    low, high = (spectra_of(table, src[...]) for table in tables)
    first = own_place()[0] == 0
    keep_ref[0:FREQS] = jnp.where(first, low, high)
    send_ref[0:FREQS] = jnp.where(first, high, low)
    place = place_of(pos[...], ang[...])
    keep_ref[FREQS : FREQS + 8] = place
    send_ref[FREQS : FREQS + 8] = place


def radiate_kernel(
    mine_ref, other_ref, pts_ref, out_ref, w_ref, cols_ref, fa_ref, fb_ref, block, sems
):
    m0 = BIN0 + own_place()[0].astype(F32)
    turn_scale = m0 * (1.0 / SAMPLES)
    tiles = pts_ref.shape[1] // OBS_TILE

    def lanes_of(rows, at):
        a, b = mine_ref[rows, at : at + OWN], other_ref[rows, at : at + OWN]
        return jnp.concatenate([a, b, a, b], axis=1)

    place = lanes_of(slice(FREQS, FREQS + 8), 0)
    pos = [place[d : d + 1] for d in range(3)]
    s, c = sin_cos(place[3:5])
    normal = [s[0:1] * c[1:2], s[0:1] * s[1:2], c[0:1]]
    size2 = RADIUS * RADIUS + (pos[0] * pos[0] + pos[1] * pos[1] + pos[2] * pos[2])
    facing = pos[0] * normal[0] + pos[1] * normal[1] + pos[2] * normal[2]
    back = [-2.0 * v for v in pos]
    cols_ref[...] = jnp.concatenate(back + [size2] * 5, axis=0).T

    def doubled(first, rest):
        return jnp.concatenate([v for v in [first] + rest for _ in range(2)], axis=0)

    shape = (8, 2 * PAIR)
    odd = (lax.broadcasted_iota(jnp.int32, shape, 0) & 1) == 1
    right = lax.broadcasted_iota(jnp.int32, shape, 1) >= PAIR
    same = odd == right
    sign_a = jnp.where(odd & ~right, 1.0, -1.0)
    sign_b = jnp.where(right & ~odd, -1.0, 1.0)
    g = doubled(size2, back) * sign_a
    h = doubled(-facing, normal)
    h_a, h_b = h * sign_a, h * sign_b
    q = lanes_of(slice(0, FREQS), 0)
    ld = lanes_of(slice(0, FREQS), OWN)
    def weights():
        for n in range(BINS):
            k = (m0 + 2.0 * n) * (2.0 * math.pi / SAMPLES)
            qr, qi = q[n : n + 1], q[BINS + n : BINS + n + 1]
            lr, li = ld[n : n + 1], ld[BINS + n : BINS + n + 1]
            turned = jnp.where(same, li, lr)
            w0 = k * (jnp.where(same, qi, qr) * g) + jnp.where(same, lr, li) * h_b
            w1 = k * (turned * h_a)
            for i, w in enumerate((w0, w1)):
                hi = w.astype(BF16)
                lo = (w - hi.astype(F32)).astype(BF16)
                w_ref[n, :, i * 128 : (i + 1) * 128] = jnp.concatenate([hi, lo], axis=0)
            yield

    def point_rows(t):
        lanes = slice(t * OBS_TILE, (t + 1) * OBS_TILE)
        return [pts_ref[d : d + 1, lanes] for d in range(3)]

    def functions(t, f_ref):
        for s in range(PAIR // ROWS):
            for half in range(OBS_TILE // FN_LANES):
                yield from functions_of(t, f_ref, s, slice(half * FN_LANES, (half + 1) * FN_LANES))

    def functions_of(t, f_ref, s, cut):
        px, py, pz = (v[:, cut] for v in point_rows(t))
        at = s * ROWS
        cx, cy, cz, c2 = (cols_ref[at : at + ROWS, d : d + 1] for d in range(4))
        r2 = c2 + (cx * px + cy * py + cz * pz)
        inv = lax.rsqrt(r2)
        r = r2 * inv
        turns = near(r * turn_scale)
        u = turns * turns
        sn = turns * horner(SIN_HALF, u)
        cs = horner(COS_HALF, u)
        inv3 = inv * inv * inv
        a0 = inv3 - inv3 * (sn * sn)
        b0 = -(inv3 * (sn * cs))
        y = r - RADIUS
        two_cos = horner(COS_STEP, y)
        sin1 = horner(SIN_STEP, y)
        cos1 = 0.5 * two_cos
        a1 = a0 * cos1 + b0 * sin1
        b1 = b0 * cos1 - a0 * sin1
        for n in range(BINS):
            for i, v in enumerate((a0, b0, a0 * r, b0 * r)):
                f_ref[n, i * PAIR + at : i * PAIR + at + ROWS, cut] = v.astype(BF16)
            if n < BINS - 2:
                a0, b0, a1, b1 = a1, b1, two_cos * a1 - a0, two_cos * b1 - b0
            else:
                a0, b0 = a1, b1
            yield

    upper = lax.broadcasted_iota(jnp.int32, (8, OBS_TILE), 0) < 4
    inner = (lax.broadcasted_iota(jnp.int32, (8, OBS_TILE), 0) & 2) == 0
    blocks = OBS_TILE // 128

    def sums(t, f_ref):
        mix = mix_of(t)
        outs = []
        for j in range(GROUPS):
            got = []
            for i in range(4):
                acc = jnp.dot(w_ref[4 * j + i], f_ref[4 * j + i], preferred_element_type=F32)
                v = (acc[0:8] + acc[8:16]) * mix
                got.append(v + pltpu.roll(v, 4, 0))
                yield
            ab = jnp.where(upper, got[0], got[2])
            cd = jnp.where(upper, got[1], got[3])
            outs.append(jnp.where(inner, ab + pltpu.roll(ab, 6, 0), cd + pltpu.roll(cd, 2, 0)))
            if j % 2 == 1:
                both = jnp.concatenate(outs[-2:], axis=0).astype(BF16)
                for b in range(blocks):
                    block[t, b, 8 * j - 8 : 8 * j + 8] = both[:, b * 128 : (b + 1) * 128]

    def mix_of(t):
        px, py, pz = point_rows(t)
        ones = jnp.ones((1, OBS_TILE), F32)
        return jnp.concatenate([ones, ones, px, px, py, py, pz, pz], axis=0)

    copies = []

    def send(t):
        copy = pltpu.make_async_copy(block.at[t], out_ref.at[pl.ds(t * blocks, blocks)], sems.at[t])
        copy.start()
        copies.append(copy)

    scratch = (fa_ref, fb_ref)
    made = functions(0, fa_ref)
    for _ in weights():
        for _ in range((PAIR // ROWS) * (OBS_TILE // FN_LANES)):
            next(made, None)
    for _ in made:
        pass
    for t in range(tiles):
        made = functions(t + 1, scratch[(t + 1) % 2]) if t + 1 < tiles else iter(())
        per_bin = (PAIR // ROWS) * (OBS_TILE // FN_LANES)
        for _ in sums(t, scratch[t % 2]):
            for _ in range(per_bin):
                next(made, None)
        for _ in made:
            pass
        send(t)
    for copy in copies:
        copy.wait()


def rays_kernel(absorb_ref, count_ref, layer_ref, length_ref, weight_ref, ground_ref, keep_ref, send_ref):
    core, group = own_place()
    own = absorb_ref[pl.ds(pl.multiple_of(group * 8, 8), 8), :]
    even = [own[2 * i : 2 * i + 1] for i in range(4)]
    odds = [own[2 * i + 1 : 2 * i + 2] for i in range(4)]
    first = core == 0
    rows8 = jnp.concatenate(
        [jnp.where(first, a, b) for a, b in zip(even, odds)]
        + [jnp.where(first, b, a) for a, b in zip(even, odds)],
        axis=0,
    )
    segs, rows = layer_ref.shape
    tile = 1024
    for q in range(rows // tile):
        lanes = slice(q * tile, (q + 1) * tile)
        count = count_ref[0:1, lanes]
        ids = lax.broadcasted_iota(jnp.int32, (LAYERS, tile), 0)
        lengths = jnp.zeros((LAYERS, tile), F32)
        for s in range(segs):
            used = jnp.where(count > s, length_ref[s : s + 1, lanes], 0.0)
            lengths = lengths + jnp.where(layer_ref[s : s + 1, lanes] == ids, used, 0.0)
        depth = jnp.dot(rows8, lengths, preferred_element_type=F32, precision=lax.Precision.HIGHEST)
        gain = weight_ref[0:1, lanes] * jnp.exp(-depth)
        ground = jnp.broadcast_to(ground_ref[0:1, lanes].astype(F32), (4, tile))
        keep_ref[:, lanes] = jnp.concatenate([gain[0:4], ground], axis=0)
        send_ref[:, lanes] = jnp.concatenate([gain[4:8], ground], axis=0)


def spots_kernel(mine_ref, other_ref, gain_ref, high_ref, low_ref):
    rows = mine_ref.shape[1]
    half = lax.shift_right_logical(lax.broadcasted_iota(jnp.int32, (8, 128), 0), 2)
    spots = lax.broadcasted_iota(jnp.int32, (128, 128), 1)
    for side, ref in enumerate((mine_ref, other_ref)):
        for q in range(rows // 128):
            block = ref[:, q * 128 : (q + 1) * 128]
            at = slice(side * rows + q * 128, side * rows + (q + 1) * 128)
            gain_ref[:, at] = jnp.concatenate([block[0:4], block[0:4]], axis=0)
            ground = jnp.concatenate([block[4:8], block[4:8]], axis=0).astype(jnp.int32)
            high = (lax.shift_right_logical(ground, 7) - half).astype(F32)
            high_ref[:, at] = jnp.concatenate([high, high], axis=0).astype(BF16)
            low = (ground & 127).astype(F32).T.astype(jnp.int32)
            low_ref[at, :] = jnp.where(low[:, 0:1] == spots, 1.0, 0.0).astype(BF16)


def ground_kernel(recv_ref, gain_ref, high_ref, low_ref, spec_ref, out_ref, z_ref, both_ref, sems):
    total = recv_ref[0].astype(F32)
    for d in range(1, recv_ref.shape[0]):
        total = total + recv_ref[d].astype(F32)
    total = (total[0:8] + total[8:16]) * (RADIUS * GAIN / math.sqrt(PANELS))
    first = own_place()[0] == 0
    turned = pltpu.roll(total, RAYS, 1)
    total = jnp.where(first, total, turned)
    spec_ref[...] = total
    sq = total * total
    power = jnp.concatenate([sq[2 * i : 2 * i + 1] + sq[2 * i + 1 : 2 * i + 2] for i in range(4)] * 2, axis=0)
    left = lax.broadcasted_iota(jnp.int32, (8, 128), 1) < RAYS
    nothing = jnp.zeros((16, 128), BF16)
    rows = gain_ref.shape[1]
    cut = 1024
    res = None
    for k in range(rows // cut):
        for q in range(k * cut // 128, (k + 1) * cut // 128):
            at = slice(q * 128, (q + 1) * 128)
            p = jnp.where(left, power[:, 2 * q : 2 * q + 1], power[:, 2 * q + 1 : 2 * q + 2])
            e = p * gain_ref[:, at]
            hi = e.astype(BF16).astype(F32)
            both = jnp.concatenate([hi, e - hi], axis=0).astype(BF16)
            high = high_ref[:, at]
            for b in range(GROUND // 256):
                z_ref[b * 16 : (b + 1) * 16, at] = jnp.where(high == float(2 * b), both, nothing)
        ks = slice(k * cut, (k + 1) * cut)
        got = jnp.dot(z_ref[:, ks], low_ref[ks, :], preferred_element_type=F32)
        res = got if res is None else res + got
    for b in range(GROUND // 256):
        v = res[b * 16 : b * 16 + 8] + res[b * 16 + 8 : b * 16 + 16]
        both_ref[b] = jnp.concatenate([v, v], axis=0).astype(BF16)
    copies = [
        pltpu.make_async_copy(both_ref, out_ref.at[:, pl.ds(j * 16, 16)], sems.at[j]) for j in range(GROUPS // 2)
    ]
    for copy in copies:
        copy.start()
    for copy in copies:
        copy.wait()


def owners_kernel(recv_ref, keep_ref, send_ref):
    first = own_place()[0] == 0
    for pair in range(GROUPS // 2):
        total = recv_ref[pair].astype(F32)
        for b in range(1, GROUND // 256):
            total = total + recv_ref[b * (GROUPS // 2) + pair].astype(F32)
        for i in range(2):
            low, high = total[i * 8 : i * 8 + 4], total[i * 8 + 4 : i * 8 + 8]
            at = (2 * pair + i) * 4
            keep_ref[at : at + 4] = jnp.where(first, low, high)
            send_ref[at : at + 4] = jnp.where(first, high, low)


def finish_kernel(keep_ref, other_ref, out_ref):
    first = own_place()[0] == 0
    keep, other = keep_ref[...], other_ref[...]
    out_ref[pl.ds(0, BINS, stride=2), :] = jnp.where(first, keep, other)
    out_ref[pl.ds(1, BINS, stride=2), :] = jnp.where(first, other, keep)


def call(body, out, scratch=(), vm=32, flops=10**6, name=None, far=(), far_out=()):
    def run(*args):
        def spec(i, places):
            return pl.BlockSpec(memory_space=pl.ANY if i in places else pltpu.VMEM)

        return pl.pallas_call(
            body,
            out_shape=out,
            in_specs=[spec(i, far) for i in range(len(args))],
            out_specs=tuple(spec(i, far_out) for i in range(len(out))),
            scratch_shapes=list(scratch),
            compiler_params=pltpu.CompilerParams(vmem_limit_bytes=vm * 1024 * 1024),
            cost_estimate=pl.CostEstimate(flops=flops, bytes_accessed=10**6, transcendentals=0),
            name=name,
        )(*args)

    return run


def struct(*shape, dtype=F32):
    return jax.ShapeDtypeStruct(shape, dtype)


def swap(value):
    return lax.ppermute(value, "panel", [(i, i ^ 1) for i in range(SHARDS)])


def between_chips(value):
    groups = [
        [(2 * b + c) * GROUPS + j for b in range(SHARDS // 2) for j in range(GROUPS)] for c in range(2)
    ]
    value = value.reshape(CHIPS, 8, 128)
    return lax.all_to_all(
        value, ("panel", "freq"), 0, 0, axis_index_groups=groups, tiled=True
    ).reshape(CHIPS // 2, 16, 128)


def shards(
    sources,
    panel_pos,
    normal_angles,
    observer_angles,
    absorption,
    ray_count,
    ray_layer,
    ray_length,
    ray_weight,
    ray_ground,
):
    obs = observer_angles.shape[1]
    rays = ray_count.shape[0]
    core = lax.rem(lax.axis_index("panel"), 2)

    with jax.named_scope("prepare"):
        keep, send, points = call(
            prepare_kernel,
            (pltpu.VMEM((FREQS + 8, PAIR), F32), pltpu.VMEM((FREQS + 8, PAIR), F32), pltpu.VMEM((8, obs), F32)),
            scratch=[
                pltpu.VMEM(sources.shape, BF16),
                pltpu.VMEM(panel_pos.shape, F32),
                pltpu.VMEM(normal_angles.shape, F32),
                pltpu.VMEM(observer_angles.shape, F32),
                pltpu.SemaphoreType.DMA((5,)),
            ],
            vm=58,
            flops=10**7,
            name="prepare",
            far=(0, 1, 2, 3),
        )(sources, panel_pos, normal_angles, observer_angles)
        other = swap(send)
    with jax.named_scope("rays"):
        gain, gain_send = call(rays_kernel, (struct(8, rays),) * 2, flops=10**7, name="rays")(
            absorption,
            ray_count.reshape(1, rays),
            ray_layer,
            ray_length,
            ray_weight.reshape(1, rays),
            ray_ground.reshape(1, rays),
        )
        gain_other = swap(gain_send)
    with jax.named_scope("radiate"):
        (partial_obs,) = call(
            radiate_kernel,
            (struct(obs // 128, FREQS, 128, dtype=BF16),),
            scratch=[
                pltpu.VMEM((BINS, 16, 4 * PAIR), BF16),
                pltpu.VMEM((2 * PAIR, 8), F32),
                pltpu.VMEM((BINS, 4 * PAIR, OBS_TILE), BF16),
                pltpu.VMEM((BINS, 4 * PAIR, OBS_TILE), BF16),
                pltpu.VMEM((obs // OBS_TILE, OBS_TILE // 128, FREQS, 128), BF16),
                pltpu.SemaphoreType.DMA((obs // OBS_TILE,)),
            ],
            vm=40,
            flops=10**9,
            name="radiate",
            far_out=(0,),
        )(keep, other, points)
    with jax.named_scope("observers_to_owners"):
        recv = between_chips(partial_obs)
    with jax.named_scope("spots"):
        spots = call(
            spots_kernel,
            (struct(8, 2 * rays), struct(16, 2 * rays, dtype=BF16), struct(2 * rays, 128, dtype=BF16)),
            flops=10**7,
            name="spots",
        )(gain, gain_other)
    with jax.named_scope("ground"):
        spectrum, ground_part = call(
            ground_kernel,
            (struct(8, 128), struct(GROUND // 256, FREQS, 128, dtype=BF16)),
            scratch=[
                pltpu.VMEM((256, 2 * rays), BF16),
                pltpu.VMEM((GROUND // 256, 16, 128), BF16),
                pltpu.SemaphoreType.DMA((GROUPS // 2,)),
            ],
            name="ground",
            far_out=(1,),
        )(recv, *spots)
    with jax.named_scope("ground_to_owners"):
        got = between_chips(ground_part)
        keep, send = call(owners_kernel, (struct(BINS, 128),) * 2, name="owners")(got)
        other = swap(send)
        (ground_power,) = call(finish_kernel, (struct(FREQS, 128),), name="finish")(keep, other)
    with jax.named_scope("spectrum"):
        mine = spectrum[:, 0:RAYS]
        other = swap(spectrum[:, RAYS:])
        even = jnp.where(core == 0, mine, other).reshape(4, 2, RAYS)
        odds = jnp.where(core == 0, other, mine).reshape(4, 2, RAYS)
        obs_spectrum = jnp.stack([even, odds], axis=1).reshape(16, RAYS).T
    return (obs_spectrum, ground_power)


def solution(mesh):
    return jax.shard_map(
        shards,
        mesh=mesh,
        in_specs=(
            P(None, ("panel", "freq"), None),
            P(None, "panel"),
            P(None, "panel"),
            P(),
            P(),
            P("panel"),
            P(None, "panel"),
            P(None, "panel"),
            P("panel"),
            P("panel"),
        ),
        out_specs=(P("panel", "freq"), P(None, "panel")),
        check_vma=False,
    )
```

```python
import math

import jax
import jax.numpy as jnp
import numpy as np
from jax import lax
from jax.experimental import pallas as pl
from jax.experimental.pallas import tpu as pltpu
from jax.sharding import PartitionSpec as P

SAMPLES = 1024
FREQS = 64
BIN0 = 32
RAYS = 64
LAYERS = 16
GROUND = 4096
RADIUS = 150.0
GAIN = 3.0
PANELS = 8192
SHARDS = 32
GROUPS = 8
CHIPS = SHARDS * GROUPS // 2
BINS = FREQS // 2
OWN = PANELS // (SHARDS * GROUPS)
PAIR = 2 * OWN
OBS_TILE = 256
FN_LANES = 256
ROWS = 16

F32 = jnp.float32
BF16 = jnp.bfloat16

SIN_HALF = (4.442882919124344, -7.308245686509013, 3.606354218431859, -0.8461116503677496, 0.10982451641401066)
COS_HALF = (1.4142134962552282, -6.978850948563772, 5.739460376906372, -1.883557905981734, 0.31068802751700825)
COS_STEP = (
    -0.53342551167462, -0.023654623427363474, 4.016642697431393e-05, 5.937236542349045e-07,
    -5.040166110800607e-10, -4.470245655063533e-12, 2.492488156438906e-15, 1.5819745095405966e-17,
)
SIN_STEP = (
    0.9637760598779563, -0.0032730579567440193, -7.257140853115864e-05, 8.21527316453533e-08,
    9.10641004058044e-10, -6.185417897022673e-13, -4.503347445205572e-15, 2.188956532785521e-18,
)


def horner(coeffs, x):
    value = x * coeffs[-1] + coeffs[-2]
    for c in coeffs[-3::-1]:
        value = value * x + c
    return value


def sin_cos(angle):
    return turn_sin_cos(angle * (0.5 / math.pi))


def turn_sin_cos(t):
    u = t * t
    s = t * horner(SIN_HALF, u)
    return s * horner(COS_HALF, u), 1.0 - s * s


def own_place():
    return lax.rem(lax.axis_index("panel"), 2), lax.axis_index("freq")


def near(turns):
    return turns - ((turns + 12582912.0) - 12582912.0)


def spectra_of(table, series):
    return lax.dot_general(
        table, series.reshape(PAIR, SAMPLES), (((1,), (1,)), ((), ())), preferred_element_type=F32
    )


def place_of(pos, ang):
    width = pos.shape[1]
    place = jnp.concatenate([pos, ang, jnp.zeros((3, width), F32)], axis=0)
    shift = lax.rem(width - OWN * own_place()[1], width)
    return pltpu.roll(place, shift, 1)[:, 0:PAIR]


def prepare_kernel(src_ref, pos_ref, ang_ref, obs_ref, keep_ref, send_ref, pts_ref, src, pos, ang, obs, sems):
    copies = [
        pltpu.make_async_copy(a, b, sems.at[i])
        for i, (a, b) in enumerate(
            [(obs_ref, obs), (src_ref.at[0], src.at[0]), (src_ref.at[1], src.at[1]), (pos_ref, pos), (ang_ref, ang)]
        )
    ]
    for copy in copies:
        copy.start()

    sample = lax.broadcasted_iota(jnp.int32, (1, SAMPLES), 1).astype(F32)
    window = (0.5 - 0.5 * turn_sin_cos(near(sample * (1.0 / SAMPLES)))[1]) * (1.0 / math.sqrt(SAMPLES))
    bins = lax.broadcasted_iota(jnp.int32, (BINS, SAMPLES), 0).astype(F32)
    tables = []
    for parity in range(2):
        turns = ((2.0 * bins + float(BIN0 + parity)) * sample) * (1.0 / SAMPLES)
        sn, cs = turn_sin_cos(near(turns))
        tables.append(jnp.concatenate([window * cs, -(window * sn)], axis=0).astype(BF16))

    copies[0].wait()
    s, c = sin_cos(obs[...])
    pts_ref[0:1] = RADIUS * s[0:1] * c[1:2]
    pts_ref[1:2] = RADIUS * s[0:1] * s[1:2]
    pts_ref[2:3] = -RADIUS * c[0:1]

    for copy in copies[1:]:
        copy.wait()
    low, high = (spectra_of(table, src[...]) for table in tables)
    first = own_place()[0] == 0
    keep_ref[0:FREQS] = jnp.where(first, low, high)
    send_ref[0:FREQS] = jnp.where(first, high, low)
    place = place_of(pos[...], ang[...])
    keep_ref[FREQS : FREQS + 8] = place
    send_ref[FREQS : FREQS + 8] = place


def radiate_kernel(
    mine_ref, other_ref, pts_ref, out_ref, w_ref, cols_ref, fa_ref, fb_ref, block, sems
):
    m0 = BIN0 + own_place()[0].astype(F32)
    turn_scale = m0 * (1.0 / SAMPLES)
    tiles = pts_ref.shape[1] // OBS_TILE

    def lanes_of(rows, at):
        a, b = mine_ref[rows, at : at + OWN], other_ref[rows, at : at + OWN]
        return jnp.concatenate([a, b, a, b], axis=1)

    place = lanes_of(slice(FREQS, FREQS + 8), 0)
    pos = [place[d : d + 1] for d in range(3)]
    s, c = sin_cos(place[3:5])
    normal = [s[0:1] * c[1:2], s[0:1] * s[1:2], c[0:1]]
    size2 = RADIUS * RADIUS + (pos[0] * pos[0] + pos[1] * pos[1] + pos[2] * pos[2])
    facing = pos[0] * normal[0] + pos[1] * normal[1] + pos[2] * normal[2]
    back = [-2.0 * v for v in pos]
    cols_ref[...] = jnp.concatenate(back + [size2] * 5, axis=0).T

    def doubled(first, rest):
        return jnp.concatenate([v for v in [first] + rest for _ in range(2)], axis=0)

    shape = (8, 2 * PAIR)
    odd = (lax.broadcasted_iota(jnp.int32, shape, 0) & 1) == 1
    right = lax.broadcasted_iota(jnp.int32, shape, 1) >= PAIR
    same = odd == right
    sign_a = jnp.where(odd & ~right, 1.0, -1.0)
    sign_b = jnp.where(right & ~odd, -1.0, 1.0)
    g = doubled(size2, back) * sign_a
    h = doubled(-facing, normal)
    h_a, h_b = h * sign_a, h * sign_b
    q = lanes_of(slice(0, FREQS), 0)
    ld = lanes_of(slice(0, FREQS), OWN)
    def weights():
        for n in range(BINS):
            k = (m0 + 2.0 * n) * (2.0 * math.pi / SAMPLES)
            qr, qi = q[n : n + 1], q[BINS + n : BINS + n + 1]
            lr, li = ld[n : n + 1], ld[BINS + n : BINS + n + 1]
            turned = jnp.where(same, li, lr)
            w0 = k * (jnp.where(same, qi, qr) * g) + jnp.where(same, lr, li) * h_b
            w1 = k * (turned * h_a)
            for i, w in enumerate((w0, w1)):
                hi = w.astype(BF16)
                lo = (w - hi.astype(F32)).astype(BF16)
                w_ref[n, :, i * 128 : (i + 1) * 128] = jnp.concatenate([hi, lo], axis=0)
            yield

    def point_rows(t):
        lanes = slice(t * OBS_TILE, (t + 1) * OBS_TILE)
        return [pts_ref[d : d + 1, lanes] for d in range(3)]

    def functions(t, f_ref):
        for s in range(PAIR // ROWS):
            for half in range(OBS_TILE // FN_LANES):
                yield from functions_of(t, f_ref, s, slice(half * FN_LANES, (half + 1) * FN_LANES))

    def functions_of(t, f_ref, s, cut):
        px, py, pz = (v[:, cut] for v in point_rows(t))
        at = s * ROWS
        cx, cy, cz, c2 = (cols_ref[at : at + ROWS, d : d + 1] for d in range(4))
        r2 = c2 + (cx * px + cy * py + cz * pz)
        inv = lax.rsqrt(r2)
        r = r2 * inv
        turns = near(r * turn_scale)
        u = turns * turns
        sn = turns * horner(SIN_HALF, u)
        cs = horner(COS_HALF, u)
        inv3 = inv * inv * inv
        a0 = inv3 - inv3 * (sn * sn)
        b0 = -(inv3 * (sn * cs))
        y = r - RADIUS
        two_cos = horner(COS_STEP, y)
        sin1 = horner(SIN_STEP, y)
        cos1 = 0.5 * two_cos
        a1 = a0 * cos1 + b0 * sin1
        b1 = b0 * cos1 - a0 * sin1
        for n in range(BINS):
            for i, v in enumerate((a0, b0, a0 * r, b0 * r)):
                f_ref[n, i * PAIR + at : i * PAIR + at + ROWS, cut] = v.astype(BF16)
            if n < BINS - 2:
                a0, b0, a1, b1 = a1, b1, two_cos * a1 - a0, two_cos * b1 - b0
            else:
                a0, b0 = a1, b1
            yield

    upper = lax.broadcasted_iota(jnp.int32, (8, OBS_TILE), 0) < 4
    inner = (lax.broadcasted_iota(jnp.int32, (8, OBS_TILE), 0) & 2) == 0
    blocks = OBS_TILE // 128

    def sums(t, f_ref):
        mix = mix_of(t)
        outs = []
        for j in range(GROUPS):
            got = []
            for i in range(4):
                acc = jnp.dot(w_ref[4 * j + i], f_ref[4 * j + i], preferred_element_type=F32)
                v = (acc[0:8] + acc[8:16]) * mix
                got.append(v + pltpu.roll(v, 4, 0))
                yield
            ab = jnp.where(upper, got[0], got[2])
            cd = jnp.where(upper, got[1], got[3])
            outs.append(jnp.where(inner, ab + pltpu.roll(ab, 6, 0), cd + pltpu.roll(cd, 2, 0)))
            if j % 2 == 1:
                both = jnp.concatenate(outs[-2:], axis=0).astype(BF16)
                for b in range(blocks):
                    block[t, b, 8 * j - 8 : 8 * j + 8] = both[:, b * 128 : (b + 1) * 128]

    def mix_of(t):
        px, py, pz = point_rows(t)
        ones = jnp.ones((1, OBS_TILE), F32)
        return jnp.concatenate([ones, ones, px, px, py, py, pz, pz], axis=0)

    copies = []

    def send(t):
        copy = pltpu.make_async_copy(block.at[t], out_ref.at[pl.ds(t * blocks, blocks)], sems.at[t])
        copy.start()
        copies.append(copy)

    scratch = (fa_ref, fb_ref)
    made = functions(0, fa_ref)
    for _ in weights():
        for _ in range((PAIR // ROWS) * (OBS_TILE // FN_LANES)):
            next(made, None)
    for _ in made:
        pass
    for t in range(tiles):
        made = functions(t + 1, scratch[(t + 1) % 2]) if t + 1 < tiles else iter(())
        per_bin = (PAIR // ROWS) * (OBS_TILE // FN_LANES)
        for _ in sums(t, scratch[t % 2]):
            for _ in range(per_bin):
                next(made, None)
        for _ in made:
            pass
        send(t)
    for copy in copies:
        copy.wait()


def rays_kernel(absorb_ref, count_ref, layer_ref, length_ref, weight_ref, ground_ref, keep_ref, send_ref):
    core, group = own_place()
    own = absorb_ref[pl.ds(pl.multiple_of(group * 8, 8), 8), :]
    even = [own[2 * i : 2 * i + 1] for i in range(4)]
    odds = [own[2 * i + 1 : 2 * i + 2] for i in range(4)]
    first = core == 0
    rows8 = jnp.concatenate(
        [jnp.where(first, a, b) for a, b in zip(even, odds)]
        + [jnp.where(first, b, a) for a, b in zip(even, odds)],
        axis=0,
    )
    segs, rows = layer_ref.shape
    tile = 1024
    for q in range(rows // tile):
        lanes = slice(q * tile, (q + 1) * tile)
        count = count_ref[0:1, lanes]
        ids = lax.broadcasted_iota(jnp.int32, (LAYERS, tile), 0)
        lengths = jnp.zeros((LAYERS, tile), F32)
        for s in range(segs):
            used = jnp.where(count > s, length_ref[s : s + 1, lanes], 0.0)
            lengths = lengths + jnp.where(layer_ref[s : s + 1, lanes] == ids, used, 0.0)
        depth = jnp.dot(rows8, lengths, preferred_element_type=F32, precision=lax.Precision.HIGHEST)
        gain = weight_ref[0:1, lanes] * jnp.exp(-depth)
        ground = jnp.broadcast_to(ground_ref[0:1, lanes].astype(F32), (4, tile))
        keep_ref[:, lanes] = jnp.concatenate([gain[0:4], ground], axis=0)
        send_ref[:, lanes] = jnp.concatenate([gain[4:8], ground], axis=0)


def spots_kernel(mine_ref, other_ref, gain_ref, high_ref, low_ref):
    rows = mine_ref.shape[1]
    spots = lax.broadcasted_iota(jnp.int32, (128, 256), 1)
    for side, ref in enumerate((mine_ref, other_ref)):
        for q in range(rows // 128):
            block = ref[:, q * 128 : (q + 1) * 128]
            at = slice(side * rows + q * 128, side * rows + (q + 1) * 128)
            gain_ref[:, at] = jnp.concatenate([block[0:4], block[0:4]], axis=0)
            ground = jnp.concatenate([block[4:8], block[4:8]], axis=0).astype(jnp.int32)
            high = lax.shift_right_logical(ground, 8).astype(F32)
            high_ref[:, at] = jnp.concatenate([high, high - 1.0], axis=0).astype(BF16)
            low = (ground & 255).astype(F32).T.astype(jnp.int32)
            low_ref[at, :] = jnp.where(low[:, 0:1] == spots, 1.0, 0.0).astype(jnp.float8_e4m3fn)


def ground_kernel(recv_ref, gain_ref, high_ref, low_ref, spec_ref, out_ref, z_ref, both_ref, sems):
    runs = [recv_ref[d].astype(F32) for d in range(4)]
    for d in range(4, recv_ref.shape[0]):
        runs[d % 4] = runs[d % 4] + recv_ref[d].astype(F32)
    total = (runs[0] + runs[1]) + (runs[2] + runs[3])
    total = (total[0:8] + total[8:16]) * (RADIUS * GAIN / math.sqrt(PANELS))
    first = own_place()[0] == 0
    turned = pltpu.roll(total, RAYS, 1)
    total = jnp.where(first, total, turned)
    spec_ref[...] = total
    sq = total * total
    power = jnp.concatenate([sq[2 * i : 2 * i + 1] + sq[2 * i + 1 : 2 * i + 2] for i in range(4)] * 2, axis=0)
    left = lax.broadcasted_iota(jnp.int32, (8, 128), 1) < RAYS
    upper = lax.broadcasted_iota(jnp.int32, (8, 128), 0) < 4
    nothing = jnp.zeros((16, 128), BF16)
    rows = gain_ref.shape[1]
    cut = 1024
    res = None
    for k in range(rows // cut):
        for q in range(k * cut // 128, (k + 1) * cut // 128):
            at = slice(q * 128, (q + 1) * 128)
            p = jnp.where(left, power[:, 2 * q : 2 * q + 1], power[:, 2 * q + 1 : 2 * q + 2])
            e = p * gain_ref[:, at]
            hi = e.astype(BF16).astype(F32)
            split = jnp.where(upper, hi, e - hi)
            both = jnp.concatenate([split, split], axis=0).astype(BF16)
            high = high_ref[:, at]
            for b in range(GROUND // 512):
                z_ref[b * 16 : (b + 1) * 16, at] = jnp.where(high == float(2 * b), both, nothing)
        ks = slice(k * cut, (k + 1) * cut)
        got = jnp.dot(z_ref[:, ks], low_ref[ks, :].astype(BF16), preferred_element_type=F32)
        res = got if res is None else res + got
    for b in range(GROUND // 256):
        v = res[b * 8 : b * 8 + 4] + res[b * 8 + 4 : b * 8 + 8]
        both_ref[b] = jnp.concatenate([v[:, 0:128], v[:, 128:256]] * 2, axis=0).astype(BF16)
    copies = [
        pltpu.make_async_copy(both_ref, out_ref.at[:, pl.ds(j * 16, 16)], sems.at[j]) for j in range(GROUPS // 2)
    ]
    for copy in copies:
        copy.start()
    for copy in copies:
        copy.wait()


def owners_kernel(recv_ref, keep_ref, send_ref):
    first = own_place()[0] == 0
    for pair in range(GROUPS // 2):
        total = recv_ref[pair].astype(F32)
        for b in range(1, GROUND // 256):
            total = total + recv_ref[b * (GROUPS // 2) + pair].astype(F32)
        for i in range(2):
            low, high = total[i * 8 : i * 8 + 4], total[i * 8 + 4 : i * 8 + 8]
            at = (2 * pair + i) * 4
            keep_ref[at : at + 4] = jnp.where(first, low, high)
            send_ref[at : at + 4] = jnp.where(first, high, low)


def finish_kernel(keep_ref, other_ref, out_ref):
    first = own_place()[0] == 0
    keep, other = keep_ref[...], other_ref[...]
    out_ref[pl.ds(0, BINS, stride=2), :] = jnp.where(first, keep, other)
    out_ref[pl.ds(1, BINS, stride=2), :] = jnp.where(first, other, keep)


def call(body, out, scratch=(), vm=32, flops=10**6, name=None, far=(), far_out=()):
    def run(*args):
        def spec(i, places):
            return pl.BlockSpec(memory_space=pl.ANY if i in places else pltpu.VMEM)

        return pl.pallas_call(
            body,
            out_shape=out,
            in_specs=[spec(i, far) for i in range(len(args))],
            out_specs=tuple(spec(i, far_out) for i in range(len(out))),
            scratch_shapes=list(scratch),
            compiler_params=pltpu.CompilerParams(vmem_limit_bytes=vm * 1024 * 1024),
            cost_estimate=pl.CostEstimate(flops=flops, bytes_accessed=10**6, transcendentals=0),
            name=name,
        )(*args)

    return run


def struct(*shape, dtype=F32):
    return jax.ShapeDtypeStruct(shape, dtype)


def swap(value):
    return lax.ppermute(value, "panel", [(i, i ^ 1) for i in range(SHARDS)])


def between_chips(value):
    groups = [
        [(2 * b + c) * GROUPS + j for b in range(SHARDS // 2) for j in range(GROUPS)] for c in range(2)
    ]
    value = value.reshape(CHIPS, 8, 128)
    return lax.all_to_all(
        value, ("panel", "freq"), 0, 0, axis_index_groups=groups, tiled=True
    ).reshape(CHIPS // 2, 16, 128)


def shards(
    sources,
    panel_pos,
    normal_angles,
    observer_angles,
    absorption,
    ray_count,
    ray_layer,
    ray_length,
    ray_weight,
    ray_ground,
):
    obs = observer_angles.shape[1]
    rays = ray_count.shape[0]
    core = lax.rem(lax.axis_index("panel"), 2)

    with jax.named_scope("prepare"):
        keep, send, points = call(
            prepare_kernel,
            (pltpu.VMEM((FREQS + 8, PAIR), F32), pltpu.VMEM((FREQS + 8, PAIR), F32), pltpu.VMEM((8, obs), F32)),
            scratch=[
                pltpu.VMEM(sources.shape, BF16),
                pltpu.VMEM(panel_pos.shape, F32),
                pltpu.VMEM(normal_angles.shape, F32),
                pltpu.VMEM(observer_angles.shape, F32),
                pltpu.SemaphoreType.DMA((5,)),
            ],
            vm=58,
            flops=10**7,
            name="prepare",
            far=(0, 1, 2, 3),
        )(sources, panel_pos, normal_angles, observer_angles)
        other = swap(send)
    with jax.named_scope("rays"):
        gain, gain_send = call(rays_kernel, (struct(8, rays),) * 2, flops=10**7, name="rays")(
            absorption,
            ray_count.reshape(1, rays),
            ray_layer,
            ray_length,
            ray_weight.reshape(1, rays),
            ray_ground.reshape(1, rays),
        )
        gain_other = swap(gain_send)
    with jax.named_scope("radiate"):
        (partial_obs,) = call(
            radiate_kernel,
            (struct(obs // 128, FREQS, 128, dtype=BF16),),
            scratch=[
                pltpu.VMEM((BINS, 16, 4 * PAIR), BF16),
                pltpu.VMEM((2 * PAIR, 8), F32),
                pltpu.VMEM((BINS, 4 * PAIR, OBS_TILE), BF16),
                pltpu.VMEM((BINS, 4 * PAIR, OBS_TILE), BF16),
                pltpu.VMEM((obs // OBS_TILE, OBS_TILE // 128, FREQS, 128), BF16),
                pltpu.SemaphoreType.DMA((obs // OBS_TILE,)),
            ],
            vm=40,
            flops=10**9,
            name="radiate",
            far_out=(0,),
        )(keep, other, points)
    with jax.named_scope("observers_to_owners"):
        recv = between_chips(partial_obs)
    with jax.named_scope("spots"):
        spots = call(
            spots_kernel,
            (struct(8, 2 * rays), struct(16, 2 * rays, dtype=BF16), struct(2 * rays, 256, dtype=jnp.float8_e4m3fn)),
            flops=10**7,
            name="spots",
        )(gain, gain_other)
    with jax.named_scope("ground"):
        spectrum, ground_part = call(
            ground_kernel,
            (struct(8, 128), struct(GROUND // 256, FREQS, 128, dtype=BF16)),
            scratch=[
                pltpu.VMEM((128, 2 * rays), BF16),
                pltpu.VMEM((GROUND // 256, 16, 128), BF16),
                pltpu.SemaphoreType.DMA((GROUPS // 2,)),
            ],
            name="ground",
            far_out=(1,),
        )(recv, *spots)
    with jax.named_scope("ground_to_owners"):
        got = between_chips(ground_part)
        keep, send = call(owners_kernel, (struct(BINS, 128),) * 2, name="owners")(got)
        other = swap(send)
        (ground_power,) = call(finish_kernel, (struct(FREQS, 128),), name="finish")(keep, other)
    with jax.named_scope("spectrum"):
        mine = spectrum[:, 0:RAYS]
        other = swap(spectrum[:, RAYS:])
        even = jnp.where(core == 0, mine, other).reshape(4, 2, RAYS)
        odds = jnp.where(core == 0, other, mine).reshape(4, 2, RAYS)
        obs_spectrum = jnp.stack([even, odds], axis=1).reshape(16, RAYS).T
    return (obs_spectrum, ground_power)


def solution(mesh):
    return jax.shard_map(
        shards,
        mesh=mesh,
        in_specs=(
            P(None, ("panel", "freq"), None),
            P(None, "panel"),
            P(None, "panel"),
            P(),
            P(),
            P("panel"),
            P(None, "panel"),
            P(None, "panel"),
            P("panel"),
            P("panel"),
        ),
        out_specs=(P("panel", "freq"), P(None, "panel")),
        check_vma=False,
    )
```
